32 devices in a mesh: expert: 16 (over z, x, core), tensor: 2 (over y), dp: 1.
Axes of the slice: x: 2, y: 2, z: 4, core: 2. Of those that a mesh axis runs over, the one named last changes fastest.
Arguments:
- tokens: bfloat16 [1536, 5120], P(('dp', 'expert'), 'tensor'), may hold values from -6 to 6
- routes: int32 [1536, 6], P(('dp', 'expert')), may hold values from 0 to 15, all different within a row; in each aligned block of 96 rows (0 to 95, 96 to 191, ...) at most 36 rows name the same one
- gates: float32 [1536, 6], P(('dp', 'expert')), may hold values from 0.05 to 0.6
- gate_up: bfloat16 [16, 5120, 2, 1024], P('expert', None, None, 'tensor'), may hold values from -0.078125 to 0.078125
- down_weight: bfloat16 [16, 5120, 1024], P('expert', None, 'tensor'), may hold values from -0.1875 to 0.1875
- old_map: int32 [16], replicated, may hold values from 0 to 15, each once
- new_map: int32 [16], replicated, may hold values from 0 to 15, each once
Outputs:
- mixed: bfloat16 [1536, 5120], P(('dp', 'expert'), 'tensor')
The draws below stay inside these ranges and needn't reach their ends.
Inputs may be any that keep to these rules, and one draw needn't show every extreme that they name: `routes`: each row names 6 different slots; in each aligned block of 96 rows (the rows of one index of expert) no slot is named by more than 36 rows; since each row names 6 different slots, every slot is then named by exactly 36 rows of every block. `old_map`: each expert appears exactly once. `new_map`: each expert appears exactly once.
All inputs are finite; a program needn't handle non-finite values.
Results may differ from the reference program's by a relative error of at most 0.0058.
Values may be sent and summed in bfloat16 or wider, within the bound.
A program may use at most 128 MiB of HBM per device.

```python
import math
import jax
import jax.numpy as jnp
import numpy as np
from jax import lax

D = 5120
HID = 1024
TOP = 6
TOK_DEV = 96
EXPERTS = 16
CAP = 36
TOKENS = 1536
N_EXPERT = 16


def steps_of(key, shape, cuts, low, largest):
    level, own = 1.0, jax.random.fold_in(key, 6)
    for axis_at, parts in cuts:
        steps = jnp.exp(jax.random.uniform(jax.random.fold_in(own, axis_at), (parts,), jnp.float32, low / len(cuts), largest / len(cuts)))
        level = level * jnp.repeat(steps, shape[axis_at] // parts).reshape([-1 if axis == axis_at else 1 for axis in range(len(shape))])
    return level


def shared_out(own_key, own, number, rows, amount, top, most, lean):
    sequence = jax.random.permutation(own_key, amount)
    packed, ordinary = load_shares(amount, rows * top, most, lean, True), load_shares(amount, rows * top, most, lean, False)
    places = jnp.arange(amount)

    def named(sizes, turn):
        used = int((sizes > 0).sum())
        fixed = max(1, used // 4)
        shifted = fixed + (places - fixed + turn * (used - fixed)) % max(1, amount - fixed)
        return jnp.zeros((amount,), jnp.int32).at[sequence[jnp.where(places < fixed, places, shifted)]].set(jnp.asarray(sizes, jnp.int32))

    sizes = jnp.where(number % 4 == 0, named(packed, number // 4), named(ordinary, number - number // 4 - 1))
    mixed = jax.random.permutation(jax.random.fold_in(own, 3), amount)
    donor, sink = mixed[0:amount // 2 * 2:2], mixed[1:amount // 2 * 2:2]
    slack = jnp.minimum(sizes[donor] - 1, most - sizes[sink]) // 2
    slack = jnp.where((donor == sequence[0]) | (sink == sequence[0]) | (sizes[sink] == 0), 0, jnp.maximum(slack, 0))
    shifted = jax.random.randint(jax.random.fold_in(own, 4), (amount // 2,), 0, 1 << 20) % (slack + 1)
    sizes = sizes.at[donor].add(-shifted).at[sink].add(shifted)
    members = jnp.searchsorted(jnp.cumsum(sizes), jnp.arange(rows * top), side="right").astype(jnp.int32)
    listing = members.reshape(top, rows).T
    listing = listing[jax.random.permutation(jax.random.fold_in(own, 1), rows)]
    turn = jax.random.randint(jax.random.fold_in(own, 2), (rows, 1), 0, top)
    return jnp.take_along_axis(listing, (jnp.arange(top)[None, :] + turn) % top, axis=1)


def load_shares(amount, total, most, skew, full):
    loads = [(1 << 20) // math.isqrt(rank ** skew) + 1 for rank in range(1, amount + 1)]
    largest = most if full else min(most, max(-(-total // amount), total * loads[0] // sum(loads)))
    least = 1 if total - largest >= amount - 1 else 0
    holding, spare = [largest] + [least] * (amount - 1), total - largest - least * (amount - 1)
    while spare > 0:
        candidates = [i for i in range(1, amount) if holding[i] < largest] or [i for i in range(1, amount) if holding[i] < most]
        mass, budget = sum([loads[i] for i in candidates]), spare
        for i in candidates:
            more = min(most - holding[i], max(1, budget * loads[i] // mass), spare)
            holding[i] = holding[i] + more
            spare = spare - more
    return np.array(holding)


def gaussian(stream_key, extent, width, most, split=(), held_as=jnp.bfloat16):
    drawn = width * jax.random.normal(stream_key, extent, jnp.float32)
    if split:
        drawn = drawn * steps_of(stream_key, extent, split, -0.22, 0.18)
    return jnp.clip(drawn, -most, most).astype(held_as)


def setup_inputs(seed: int = 0, part: int = 0) -> dict:
    keys = jax.random.split(jax.random.key(seed), 8)
    part_keys = jax.random.split(jax.random.fold_in(keys[7], part), 8)
    tokens = gaussian(part_keys[0], (TOKENS, D), 1.0, 6.0, ((0, 16), (1, 2)))
    routes_keys = jax.random.split(jax.random.fold_in(part_keys[1], 1), TOKENS // TOK_DEV)
    routes_turns = jax.random.permutation(jax.random.fold_in(part_keys[1], 3), TOKENS // TOK_DEV)
    routes = jax.vmap(lambda own, number: shared_out(jax.random.fold_in(part_keys[1], 2), own, number, TOK_DEV, EXPERTS, TOP, CAP, 2))(routes_keys, routes_turns).reshape((TOKENS, TOP))
    gates = jnp.clip(0.05 + 0.55 * jax.random.uniform(part_keys[2], (TOKENS, TOP), jnp.float32) ** steps_of(part_keys[2], (TOKENS, TOP), ((0, 16),), -0.2, 0.2), 0.05, 0.6)
    gate_up = gaussian(keys[3], (EXPERTS, D, 2, HID), D ** -0.5, 0.078125, ((0, 16), (3, 2)))
    down_weight = gaussian(keys[4], (EXPERTS, D, HID), HID ** -0.5, 0.1875, ((0, 16), (2, 2)))
    old_map = jax.random.permutation(keys[5], EXPERTS).astype(jnp.int32)
    new_map = jax.random.permutation(keys[6], EXPERTS).astype(jnp.int32)
    return {"tokens": tokens, "routes": routes, "gates": gates, "gate_up": gate_up, "down_weight": down_weight, "old_map": old_map, "new_map": new_map}


def reference(tokens, routes, gates, gate_up, down_weight, old_map, new_map):
    slot_ids = jnp.arange(EXPERTS, dtype=jnp.int32)
    holder = jnp.sum(jnp.where(new_map[:, None] == old_map[None, :], slot_ids[None, :], 0), axis=1).astype(jnp.int32)
    buffer_rows = N_EXPERT * CAP

    def one_slot(carry, slot):
        chosen = routes == slot
        token_gate = jnp.sum(jnp.where(chosen, gates, 0.0), axis=1)
        picked = jnp.any(chosen, axis=1)
        order = jnp.argsort(jnp.where(picked, 0, 1).astype(jnp.int32), stable=True)[:buffer_rows]
        inputs = tokens[order]
        owner = holder[slot]
        weight_in = lax.dynamic_index_in_dim(gate_up, owner, 0, keepdims=False)
        weight_out = lax.dynamic_index_in_dim(down_weight, owner, 0, keepdims=False)
        gate = jnp.dot(inputs, weight_in[:, 0, :], preferred_element_type=jnp.float32)
        up = jnp.dot(inputs, weight_in[:, 1, :], preferred_element_type=jnp.float32)
        act = (jax.nn.silu(gate) * up).astype(jnp.bfloat16)
        expert_out = jnp.dot(act, weight_out.T, preferred_element_type=jnp.float32).astype(jnp.bfloat16)
        contribution = token_gate[order][:, None] * expert_out.astype(jnp.float32)
        return carry.at[order].add(contribution), None

    mixed, _ = lax.scan(one_slot, jnp.zeros((TOKENS, D), jnp.float32), slot_ids)
    return mixed.astype(jnp.bfloat16)
```

```python
import functools

import jax
import jax.numpy as jnp
from jax import lax
from jax.experimental import pallas as pl
from jax.experimental.pallas import tpu as pltpu
from jax.sharding import PartitionSpec as P

MESH = pl.DeviceIdType.MESH
VMEM_BUDGET = 56 * 2**20


def place(zs):
    e, y = lax.axis_index("expert"), lax.axis_index("tensor")
    z, x, c = lax.div(e, 4), lax.rem(lax.div(e, 2), 2), lax.rem(e, 2)
    return z, x, y, c


def device(z, x, y, c):
    return {"expert": (z * 2 + x) * 2 + c, "tensor": y}


def greet(zs, z, x, y, c):
    barrier = pltpu.get_barrier_semaphore()

    def hello(dev):
        pl.semaphore_signal(barrier, inc=1, device_id=dev, device_id_type=MESH)

    hello(device(z, 1 - x, y, c))
    hello(device(z, x, 1 - y, c))
    hello(device(z, x, y, 1 - c))
    pl.when(z > 0)(lambda: hello(device(z - 1, x, y, c)))
    pl.when(z < zs - 1)(lambda: hello(device(z + 1, x, y, c)))
    pl.semaphore_wait(barrier, 3 + (z > 0).astype(jnp.int32) + (z < zs - 1).astype(jnp.int32))


UP, DOWN, XL, YL, SIB = range(5)


def gather_kernel(zs, rows, tok_ref, out_ref, local_sem, send_sem, recv_sem):
    z, x, y, c = place(zs)
    half = rows // 2
    greet(zs, z, x, y, c)

    def slot(pz, px, py, pc, h):
        return out_ref.at[py, pl.ds(((pz * 2 + px) * 2 + pc) * rows + h * half, half), :]

    def index(pz, px, py):
        return (pz * 2 + px) * 2 + py

    def copy(link, pz, px, py, h, own=False):
        dev = (
            device(z + 1, x, y, c),
            device(z - 1, x, y, c),
            device(z, 1 - x, y, c),
            device(z, x, 1 - y, c),
            device(z, x, y, 1 - c),
        )[link]
        src = tok_ref.at[pl.ds(h * half, half), :] if own else slot(pz, px, py, c, h)
        i = index(pz, px, py)
        return pltpu.make_async_remote_copy(
            src_ref=src,
            dst_ref=slot(pz, px, py, c, h),
            send_sem=send_sem.at[link, i, h],
            recv_sem=recv_sem.at[c, i, h],
            device_id=dev,
            device_id_type=MESH,
        )

    def arrived(pz, px, py, pc, h):
        pltpu.make_async_copy(
            slot(pz, px, py, pc, h), slot(pz, px, py, pc, h), recv_sem.at[pc, index(pz, px, py), h]
        ).wait()

    def hop(d, fu, fv, h, act):
        pz = z + d
        px = 1 - x if (fu if h == 0 else fv) else x
        py = 1 - y if (fv if h == 0 else fu) else y
        u, v = (XL, YL) if h == 0 else (YL, XL)
        own = d == 0 and not fu and not fv
        if not fu and not fv:
            if d <= 0:
                pl.when(z < zs - 1)(lambda: act(copy(UP, pz, px, py, h, own)))
            if d >= 0:
                pl.when(z > 0)(lambda: act(copy(DOWN, pz, px, py, h, own)))
        if not fu and not fv:
            act(copy(u, pz, px, py, h, own))
        if not fv:
            act(copy(v, pz, px, py, h, own))
        act(copy(SIB, pz, px, py, h, own))

    events = [
        (d, fu, fv, h)
        for d in range(-(zs - 1), zs)
        for fu in (0, 1)
        for fv in (0, 1)
        for h in (0, 1)
    ]
    events.sort(key=lambda t: (abs(t[0]) + t[1] + t[2], t[2], t[1]))
    mine = pltpu.make_async_copy(
        tok_ref, out_ref.at[y, pl.ds(((z * 2 + x) * 2 + c) * rows, rows), :], local_sem
    )
    mine.start()
    for d, fu, fv, h in events:

        def step(d=d, fu=fu, fv=fv, h=h):
            if d or fu or fv:
                px = 1 - x if (fu if h == 0 else fv) else x
                py = 1 - y if (fv if h == 0 else fu) else y
                arrived(z + d, px, py, c, h)
            hop(d, fu, fv, h, lambda k: k.start())

        if d == 0:
            step()
        else:
            pl.when((z + d >= 0) & (z + d < zs))(step)
    mine.wait()
    for pz in range(zs):
        for px in range(2):
            for py in range(2):
                for h in range(2):
                    arrived(pz, px, py, 1 - c, h)
    for d, fu, fv, h in events:

        def finish(d=d, fu=fu, fv=fv, h=h):
            hop(d, fu, fv, h, lambda k: k.wait_send())

        if d == 0:
            finish()
        else:
            pl.when((z + d >= 0) & (z + d < zs))(finish)


def scatter_kernel(zs, rows, part_ref, out_ref, acc, rv, ru, rz, send_sem, sib_sem, v_sem, u_sem, z_sem):
    z, x, y, c = place(zs)
    half = rows // 2
    greet(zs, z, x, y, c)

    def index(pz, px, py):
        return (pz * 2 + px) * 2 + py

    def mine(pz, px, py, pc, h):
        return part_ref.at[py, pl.ds(((pz * 2 + px) * 2 + pc) * rows + h * half, half), :]

    def spot(d, fu, fv, h):
        return z + d, (1 - x if (fu if h == 0 else fv) else x), (1 - y if (fv if h == 0 else fu) else y)

    def add(dst, *srcs):
        def body(i, _):
            r = pl.ds(pl.multiple_of(i * 16, 16), 16)
            total = srcs[0][r, :].astype(jnp.float32)
            for s in srcs[1:]:
                total = total + s[r, :].astype(jnp.float32)
            dst[r, :] = total.astype(dst.dtype)
            return 0

        lax.fori_loop(0, half // 16, body, 0)

    def sib_copy(pz, px, py, h):
        i = index(pz, px, py)
        return pltpu.make_async_remote_copy(
            src_ref=mine(pz, px, py, 1 - c, h),
            dst_ref=acc.at[i, h],
            send_sem=send_sem.at[0, i, h],
            recv_sem=sib_sem.at[i, h],
            device_id=device(z, x, y, 1 - c),
            device_id_type=MESH,
        )

    def v_copy(d, fu, h):
        pz, px, py = spot(d, fu, 1, h)
        i = index(pz, px, py)
        dev = device(z, x, 1 - y, c) if h == 0 else device(z, 1 - x, y, c)
        k = pz * 2 + (px if h == 0 else py)
        return pltpu.make_async_remote_copy(
            src_ref=acc.at[i, h],
            dst_ref=rv.at[k, h],
            send_sem=send_sem.at[1, i, h],
            recv_sem=v_sem.at[k, h],
            device_id=dev,
            device_id_type=MESH,
        )

    def u_copy(d, h):
        pz, px, py = spot(d, 1, 0, h)
        i = index(pz, px, py)
        dev = device(z, 1 - x, y, c) if h == 0 else device(z, x, 1 - y, c)
        return pltpu.make_async_remote_copy(
            src_ref=acc.at[i, h],
            dst_ref=ru.at[pz, h],
            send_sem=send_sem.at[2, i, h],
            recv_sem=u_sem.at[pz, h],
            device_id=dev,
            device_id_type=MESH,
        )

    def z_copy(d, h):
        pz, px, py = spot(d, 0, 0, h)
        i = index(pz, px, py)
        way = 0 if d > 0 else 1
        return pltpu.make_async_remote_copy(
            src_ref=acc.at[i, h],
            dst_ref=rz.at[way, pz, h],
            send_sem=send_sem.at[3, i, h],
            recv_sem=z_sem.at[way, pz, h],
            device_id=device(z + 1 if d > 0 else z - 1, x, y, c),
            device_id_type=MESH,
        )

    def landed(ref, sem):
        pltpu.make_async_copy(ref, ref, sem).wait()

    def when_there(d, f):
        if d == 0:
            f()
        else:
            pl.when((z + d >= 0) & (z + d < zs))(f)

    order = [[s * k for s in ((1, -1) if k else (1,))] for k in range(zs - 1, -1, -1)]
    pairs = [(fu, fv) for fv in (1, 0) for fu in (1, 0)]

    def first(ds):
        for d in ds:
            for fu, fv in pairs:
                for h in (0, 1):
                    when_there(d, lambda: sib_copy(*spot(d, fu, fv, h), h).start())

    def stage0(ds):
        for d in ds:

            def run():
                for fu, fv in pairs:
                    for h in (0, 1):
                        pz, px, py = spot(d, fu, fv, h)
                        i = index(pz, px, py)
                        landed(acc.at[i, h], sib_sem.at[i, h])
                        add(acc.at[i, h], acc.at[i, h], mine(pz, px, py, c, h))
                        if fv:
                            v_copy(d, fu, h).start()

            when_there(d, run)

    def stage1(ds):
        for d in ds:

            def run():
                for fu in (1, 0):
                    for h in (0, 1):
                        pz, px, py = spot(d, fu, 0, h)
                        i = index(pz, px, py)
                        k = pz * 2 + (px if h == 0 else py)
                        landed(rv.at[k, h], v_sem.at[k, h])
                        add(acc.at[i, h], acc.at[i, h], rv.at[k, h])
                        if fu:
                            u_copy(d, h).start()

            when_there(d, run)

    def stage2(ds):
        for d in ds:

            def run():
                for h in (0, 1):
                    pz, px, py = spot(d, 0, 0, h)
                    i = index(pz, px, py)
                    landed(ru.at[pz, h], u_sem.at[pz, h])
                    add(acc.at[i, h], acc.at[i, h], ru.at[pz, h])
                    for way, source in ((0, z > 0), (1, z < zs - 1)):
                        if (way == 0 and d < 0) or (way == 1 and d > 0):
                            continue

                        def more():
                            landed(rz.at[way, pz, h], z_sem.at[way, pz, h])
                            add(acc.at[i, h], acc.at[i, h], rz.at[way, pz, h])

                        pl.when(source)(more)
                    if d:
                        z_copy(d, h).start()
                    else:
                        add(out_ref.at[pl.ds(h * half, half), :], acc.at[i, h])

            when_there(d, run)

    for ds in order:
        first(ds)
    n = len(order)
    for t in range(n + 2):
        if t < n:
            stage0(order[t])
        if 0 <= t - 1 < n:
            stage1(order[t - 1])
        if 0 <= t - 2 < n:
            stage2(order[t - 2])
    for ds in order:
        for d in ds:

            def done():
                for h in (0, 1):
                    for fu, fv in pairs:
                        sib_copy(*spot(d, fu, fv, h), h).wait_send()
                    for fu in (0, 1):
                        v_copy(d, fu, h).wait_send()
                    u_copy(d, h).wait_send()
                    if d:
                        z_copy(d, h).wait_send()

            when_there(d, done)


def weights_of(routes, gates, old_map, new_map):
    experts = lax.axis_size("expert")
    ids = jnp.arange(experts, dtype=jnp.int32)
    holder = jnp.sum(jnp.where(new_map[:, None] == old_map[None, :], ids[None, :], 0), axis=1)
    target = jnp.sum(jnp.where(routes[:, :, None] == ids, holder, 0), axis=2)
    return jnp.sum(jnp.where(target[:, :, None] == ids, gates[:, :, None], 0.0), axis=1)


def gathered(tokens, routes, gates, gate_up, down_weight, old_map, new_map):
    experts, tensors = lax.axis_size("expert"), lax.axis_size("tensor")
    zs = experts // 4
    rows, part = tokens.shape
    _, width, _, hidden = gate_up.shape
    dma = pltpu.SemaphoreType.DMA
    mine = lax.axis_index("expert")
    table = lax.all_gather(
        weights_of(routes, gates, old_map, new_map).T, "expert", axis=1, tiled=True
    )
    share = lax.dynamic_index_in_dim(table, mine, 0, keepdims=False)[:, None]
    every = pl.pallas_call(
        functools.partial(gather_kernel, zs, rows),
        out_shape=jax.ShapeDtypeStruct((tensors, experts * rows, part), tokens.dtype),
        in_specs=[pl.BlockSpec(memory_space=pl.ANY)],
        out_specs=pl.BlockSpec(memory_space=pl.ANY),
        scratch_shapes=[dma, dma((5, zs * 4, 2)), dma((2, zs * 4, 2))],
        compiler_params=pltpu.CompilerParams(
            collective_id=0, has_side_effects=True, vmem_limit_bytes=VMEM_BUDGET
        ),
        name="gather_tokens",
    )(tokens)
    w_in = gate_up.reshape(width, 2 * hidden)
    projected = sum(
        jnp.dot(every[k], w_in[k * part : (k + 1) * part], preferred_element_type=jnp.float32)
        for k in range(tensors)
    )
    act = (jax.nn.silu(projected[:, :hidden]) * projected[:, hidden:]).astype(jnp.bfloat16)
    w_out = down_weight.reshape(tensors, part, hidden)
    partial = jnp.stack(
        [
            (
                share
                * lax.dot_general(
                    act, w_out[k], (((1,), (1,)), ((), ())), preferred_element_type=jnp.float32
                )
            ).astype(jnp.bfloat16)
            for k in range(tensors)
        ]
    )
    half = rows // 2
    return pl.pallas_call(
        functools.partial(scatter_kernel, zs, rows),
        out_shape=jax.ShapeDtypeStruct((rows, part), jnp.bfloat16),
        in_specs=[pl.BlockSpec(memory_space=pltpu.VMEM)],
        out_specs=pl.BlockSpec(memory_space=pltpu.VMEM),
        scratch_shapes=[
            pltpu.VMEM((zs * 4, 2, half, part), jnp.bfloat16),
            pltpu.VMEM((zs * 2, 2, half, part), jnp.bfloat16),
            pltpu.VMEM((zs, 2, half, part), jnp.bfloat16),
            pltpu.VMEM((2, zs, 2, half, part), jnp.bfloat16),
            dma((4, zs * 4, 2)),
            dma((zs * 4, 2)),
            dma((zs * 2, 2)),
            dma((zs, 2)),
            dma((2, zs, 2)),
        ],
        compiler_params=pltpu.CompilerParams(
            collective_id=1, has_side_effects=True, vmem_limit_bytes=VMEM_BUDGET
        ),
        name="scatter_sums",
    )(partial)


def routed(tokens, routes, gates, gate_up, down_weight, old_map, new_map):
    experts, tensors = lax.axis_size("expert"), lax.axis_size("tensor")
    rows, part = tokens.shape
    picks = routes.shape[1]
    capacity = (rows * picks + experts - 1) // experts
    _, width, _, hidden = gate_up.shape
    total = experts * capacity
    weight = weights_of(routes, gates, old_map, new_map)
    chosen = weights_of(routes, jnp.ones_like(gates), old_map, new_map)
    earlier = jnp.tril(jnp.ones((rows, rows), jnp.bfloat16), -1)
    position = jnp.dot(
        earlier, chosen.astype(jnp.bfloat16), preferred_element_type=jnp.float32
    ).astype(jnp.int32)
    hit = (position[:, :, None] == jnp.arange(capacity)) & (chosen[:, :, None] > 0)
    assign = hit.astype(jnp.bfloat16).reshape(rows, total)
    combine = jnp.where(hit, weight[:, :, None], 0.0).reshape(rows, total)
    outgoing = lax.dot_general(
        assign, tokens, (((0,), (0,)), ((), ())), preferred_element_type=jnp.float32
    )
    outgoing = outgoing.astype(jnp.bfloat16).reshape(experts, capacity, part)
    arrived = lax.all_to_all(outgoing, "expert", split_axis=0, concat_axis=0, tiled=True)
    piece = lax.all_gather(arrived, "tensor", axis=2, tiled=True).reshape(total, width)
    projected = jnp.dot(
        piece, gate_up.reshape(width, 2 * hidden), preferred_element_type=jnp.float32
    )
    act = (jax.nn.silu(projected[:, :hidden]) * projected[:, hidden:]).astype(jnp.bfloat16)
    down = lax.all_to_all(
        down_weight.reshape(tensors, part, hidden), "tensor", split_axis=0, concat_axis=2, tiled=True
    ).reshape(part, tensors * hidden)
    out = lax.dot_general(
        lax.all_gather(act, "tensor", axis=1, tiled=True),
        down,
        (((1,), (1,)), ((), ())),
        preferred_element_type=jnp.float32,
    )
    out = out.astype(jnp.bfloat16).reshape(experts, capacity, part)
    back = lax.all_to_all(out, "expert", split_axis=0, concat_axis=0, tiled=True)
    mixed = jnp.dot(
        combine,
        back.reshape(total, part).astype(jnp.float32),
        precision=lax.Precision.HIGHEST,
        preferred_element_type=jnp.float32,
    )
    return mixed.astype(jnp.bfloat16)


def local(*args):
    experts, tensors = lax.axis_size("expert"), lax.axis_size("tensor")
    rows, part = args[0].shape
    held = experts * rows * part * 2 * (tensors + 2)
    fits = tensors == 2 and experts % 4 == 0 and experts >= 8 and rows % 32 == 0
    if fits and held < VMEM_BUDGET:
        return gathered(*args)
    return routed(*args)


def solution(mesh):
    in_specs = (
        P(("dp", "expert"), "tensor"),
        P(("dp", "expert"), None),
        P(("dp", "expert"), None),
        P("expert", None, None, "tensor"),
        P("expert", None, "tensor"),
        P(),
        P(),
    )
    out_specs = P(("dp", "expert"), "tensor")
    return jax.shard_map(local, mesh=mesh, in_specs=in_specs, out_specs=out_specs, check_vma=False)
```

```python
import functools

import jax
import jax.numpy as jnp
from jax import lax
from jax.experimental import pallas as pl
from jax.experimental.pallas import tpu as pltpu
from jax.sharding import PartitionSpec as P

MESH = pl.DeviceIdType.MESH
VMEM_BUDGET = 56 * 2**20


def place(zs):
    e, y = lax.axis_index("expert"), lax.axis_index("tensor")
    z, x, c = lax.div(e, 4), lax.rem(lax.div(e, 2), 2), lax.rem(e, 2)
    return z, x, y, c


def device(z, x, y, c):
    return {"expert": (z * 2 + x) * 2 + c, "tensor": y}


def greet(zs, z, x, y, c):
    barrier = pltpu.get_barrier_semaphore()

    def hello(dev):
        pl.semaphore_signal(barrier, inc=1, device_id=dev, device_id_type=MESH)

    hello(device(z, 1 - x, y, c))
    hello(device(z, x, 1 - y, c))
    hello(device(z, x, y, 1 - c))
    pl.when(z > 0)(lambda: hello(device(z - 1, x, y, c)))
    pl.when(z < zs - 1)(lambda: hello(device(z + 1, x, y, c)))
    pl.semaphore_wait(barrier, 3 + (z > 0).astype(jnp.int32) + (z < zs - 1).astype(jnp.int32))


UP, DOWN, XL, YL, SIB = range(5)
TABLE = 2


def gather_kernel(zs, rows, tok_ref, tab_ref, out_ref, all_ref, local_sem, send_sem, recv_sem):
    z, x, y, c = place(zs)
    half = rows // 2
    part = tok_ref.shape[1]
    greet(zs, z, x, y, c)

    def slot(pz, px, py, pc, h):
        e = (pz * 2 + px) * 2 + pc
        if h == TABLE:
            return all_ref.at[e]
        columns = pl.ds(pl.multiple_of(py * part, 128), part)
        return out_ref.at[pl.ds(pl.multiple_of(e * rows + h * half, 16), half), columns]

    def index(pz, px, py):
        return (pz * 2 + px) * 2 + py

    def copy(link, pz, px, py, h, own=False):
        dev = (
            device(z + 1, x, y, c),
            device(z - 1, x, y, c),
            device(z, 1 - x, y, c),
            device(z, x, 1 - y, c),
            device(z, x, y, 1 - c),
        )[link]
        src = slot(pz, px, py, c, h)
        if own:
            src = tab_ref if h == TABLE else tok_ref.at[pl.ds(h * half, half), :]
        i = index(pz, px, py)
        return pltpu.make_async_remote_copy(
            src_ref=src,
            dst_ref=slot(pz, px, py, c, h),
            send_sem=send_sem.at[link, i, h],
            recv_sem=recv_sem.at[c, i, h],
            device_id=dev,
            device_id_type=MESH,
        )

    def arrived(pz, px, py, pc, h):
        pltpu.make_async_copy(
            slot(pz, px, py, pc, h), slot(pz, px, py, pc, h), recv_sem.at[pc, index(pz, px, py), h]
        ).wait()

    def hop(d, fu, fv, h, act):
        pz = z + d
        px = 1 - x if (fu if h == 0 else fv) else x
        py = 1 - y if (fv if h == 0 else fu) else y
        u, v = (XL, YL) if h == 0 else (YL, XL)
        own = d == 0 and not fu and not fv
        if not fu and not fv:
            if d <= 0:
                pl.when(z < zs - 1)(lambda: act(copy(UP, pz, px, py, h, own)))
            if d >= 0:
                pl.when(z > 0)(lambda: act(copy(DOWN, pz, px, py, h, own)))
        if not fu and not fv:
            act(copy(u, pz, px, py, h, own))
        if not fv:
            act(copy(v, pz, px, py, h, own))
        act(copy(SIB, pz, px, py, h, own))
        if h == 0 and not fv:
            if not fu:
                if d <= 0:
                    pl.when(z < zs - 1)(lambda: act(copy(UP, pz, px, py, TABLE, own)))
                if d >= 0:
                    pl.when(z > 0)(lambda: act(copy(DOWN, pz, px, py, TABLE, own)))
                act(copy(XL, pz, px, py, TABLE, own))
            act(copy(SIB, pz, px, py, TABLE, own))

    events = [
        (d, fu, fv, h)
        for d in range(-(zs - 1), zs)
        for fu in (0, 1)
        for fv in (0, 1)
        for h in (0, 1)
    ]
    events.sort(key=lambda t: (abs(t[0]) + t[1] + t[2], t[2], t[1]))
    e = (z * 2 + x) * 2 + c
    columns = pl.ds(pl.multiple_of(y * part, 128), part)
    mine = pltpu.make_async_copy(
        tok_ref, out_ref.at[pl.ds(pl.multiple_of(e * rows, 16), rows), columns], local_sem.at[0]
    )
    listed = pltpu.make_async_copy(tab_ref, all_ref.at[e], local_sem.at[1])
    mine.start()
    listed.start()
    for d, fu, fv, h in events:

        def step(d=d, fu=fu, fv=fv, h=h):
            if d or fu or fv:
                px = 1 - x if (fu if h == 0 else fv) else x
                py = 1 - y if (fv if h == 0 else fu) else y
                arrived(z + d, px, py, c, h)
                if h == 0 and not fv:
                    arrived(z + d, px, py, c, TABLE)
            hop(d, fu, fv, h, lambda k: k.start())

        if d == 0:
            step()
        else:
            pl.when((z + d >= 0) & (z + d < zs))(step)
    mine.wait()
    listed.wait()
    for pz in range(zs):
        for px in range(2):
            arrived(pz, px, y, 1 - c, TABLE)
            for py in range(2):
                for h in range(2):
                    arrived(pz, px, py, 1 - c, h)
    for d, fu, fv, h in events:

        def finish(d=d, fu=fu, fv=fv, h=h):
            hop(d, fu, fv, h, lambda k: k.wait_send())

        if d == 0:
            finish()
        else:
            pl.when((z + d >= 0) & (z + d < zs))(finish)


def scatter_kernel(
    zs, rows, part_ref, out_ref, acc, held, rv, ru, rz, send_sem, own_sem, sib_sem, v_sem, u_sem, z_sem
):
    z, x, y, c = place(zs)
    half = rows // 2
    part = out_ref.shape[1]
    greet(zs, z, x, y, c)

    def index(pz, px, py):
        return (pz * 2 + px) * 2 + py

    def mine(pz, px, py, pc, h):
        first_row = ((pz * 2 + px) * 2 + pc) * rows + h * half
        columns = pl.ds(pl.multiple_of(py * part, 128), part)
        return part_ref.at[pl.ds(pl.multiple_of(first_row, 16), half), columns]

    def own_copy(pz, px, py, h):
        i = index(pz, px, py)
        return pltpu.make_async_copy(mine(pz, px, py, c, h), held.at[i, h], own_sem.at[i, h])

    def spot(d, fu, fv, h):
        return z + d, (1 - x if (fu if h == 0 else fv) else x), (1 - y if (fv if h == 0 else fu) else y)

    def add(dst, *srcs):
        def body(i, _):
            r = pl.ds(pl.multiple_of(i * 16, 16), 16)
            total = srcs[0][r, :].astype(jnp.float32)
            for s in srcs[1:]:
                total = total + s[r, :].astype(jnp.float32)
            dst[r, :] = total.astype(dst.dtype)
            return 0

        lax.fori_loop(0, half // 16, body, 0)

    def sib_copy(pz, px, py, h):
        i = index(pz, px, py)
        return pltpu.make_async_remote_copy(
            src_ref=mine(pz, px, py, 1 - c, h),
            dst_ref=acc.at[i, h],
            send_sem=send_sem.at[0, i, h],
            recv_sem=sib_sem.at[i, h],
            device_id=device(z, x, y, 1 - c),
            device_id_type=MESH,
        )

    def v_copy(d, fu, h):
        pz, px, py = spot(d, fu, 1, h)
        i = index(pz, px, py)
        dev = device(z, x, 1 - y, c) if h == 0 else device(z, 1 - x, y, c)
        k = pz * 2 + (px if h == 0 else py)
        return pltpu.make_async_remote_copy(
            src_ref=acc.at[i, h],
            dst_ref=rv.at[k, h],
            send_sem=send_sem.at[1, i, h],
            recv_sem=v_sem.at[k, h],
            device_id=dev,
            device_id_type=MESH,
        )

    def u_copy(d, h):
        pz, px, py = spot(d, 1, 0, h)
        i = index(pz, px, py)
        dev = device(z, 1 - x, y, c) if h == 0 else device(z, x, 1 - y, c)
        return pltpu.make_async_remote_copy(
            src_ref=acc.at[i, h],
            dst_ref=ru.at[pz, h],
            send_sem=send_sem.at[2, i, h],
            recv_sem=u_sem.at[pz, h],
            device_id=dev,
            device_id_type=MESH,
        )

    def z_copy(d, h):
        pz, px, py = spot(d, 0, 0, h)
        i = index(pz, px, py)
        way = 0 if d > 0 else 1
        return pltpu.make_async_remote_copy(
            src_ref=acc.at[i, h],
            dst_ref=rz.at[way, pz, h],
            send_sem=send_sem.at[3, i, h],
            recv_sem=z_sem.at[way, pz, h],
            device_id=device(z + 1 if d > 0 else z - 1, x, y, c),
            device_id_type=MESH,
        )

    def landed(ref, sem):
        pltpu.make_async_copy(ref, ref, sem).wait()

    def when_there(d, f):
        if d == 0:
            f()
        else:
            pl.when((z + d >= 0) & (z + d < zs))(f)

    order = [[s * k for s in ((1, -1) if k else (1,))] for k in range(zs - 1, -1, -1)]
    pairs = [(fu, fv) for fv in (1, 0) for fu in (1, 0)]

    def first(ds):
        for d in ds:
            for fu, fv in pairs:
                for h in (0, 1):
                    when_there(d, lambda: sib_copy(*spot(d, fu, fv, h), h).start())
                    when_there(d, lambda: own_copy(*spot(d, fu, fv, h), h).start())

    def stage0(ds):
        for d in ds:

            def run():
                for fu, fv in pairs:
                    for h in (0, 1):
                        pz, px, py = spot(d, fu, fv, h)
                        i = index(pz, px, py)
                        landed(acc.at[i, h], sib_sem.at[i, h])
                        own_copy(pz, px, py, h).wait()
                        add(acc.at[i, h], acc.at[i, h], held.at[i, h])
                        if fv:
                            v_copy(d, fu, h).start()

            when_there(d, run)

    def stage1(ds):
        for d in ds:

            def run():
                for fu in (1, 0):
                    for h in (0, 1):
                        pz, px, py = spot(d, fu, 0, h)
                        i = index(pz, px, py)
                        k = pz * 2 + (px if h == 0 else py)
                        landed(rv.at[k, h], v_sem.at[k, h])
                        add(acc.at[i, h], acc.at[i, h], rv.at[k, h])
                        if fu:
                            u_copy(d, h).start()

            when_there(d, run)

    def stage2(ds):
        for d in ds:

            def run():
                for h in (0, 1):
                    pz, px, py = spot(d, 0, 0, h)
                    i = index(pz, px, py)
                    landed(ru.at[pz, h], u_sem.at[pz, h])
                    add(acc.at[i, h], acc.at[i, h], ru.at[pz, h])
                    for way, source in ((0, z > 0), (1, z < zs - 1)):
                        if (way == 0 and d < 0) or (way == 1 and d > 0):
                            continue

                        def more():
                            landed(rz.at[way, pz, h], z_sem.at[way, pz, h])
                            add(acc.at[i, h], acc.at[i, h], rz.at[way, pz, h])

                        pl.when(source)(more)
                    if d:
                        z_copy(d, h).start()
                    else:
                        add(out_ref.at[pl.ds(h * half, half), :], acc.at[i, h])

            when_there(d, run)

    for ds in order:
        first(ds)
    n = len(order)
    for t in range(n + 2):
        if t < n:
            stage0(order[t])
        if 0 <= t - 1 < n:
            stage1(order[t - 1])
        if 0 <= t - 2 < n:
            stage2(order[t - 2])
    for ds in order:
        for d in ds:

            def done():
                for h in (0, 1):
                    for fu, fv in pairs:
                        sib_copy(*spot(d, fu, fv, h), h).wait_send()
                    for fu in (0, 1):
                        v_copy(d, fu, h).wait_send()
                    u_copy(d, h).wait_send()
                    if d:
                        z_copy(d, h).wait_send()

            when_there(d, done)


def weights_of(routes, gates, old_map, new_map):
    experts = lax.axis_size("expert")
    ids = jnp.arange(experts, dtype=jnp.int32)
    holder = jnp.sum(jnp.where(new_map[:, None] == old_map[None, :], ids[None, :], 0), axis=1)
    target = jnp.sum(jnp.where(routes[:, :, None] == ids, holder, 0), axis=2)
    return jnp.sum(jnp.where(target[:, :, None] == ids, gates[:, :, None], 0.0), axis=1)


def gathered(tokens, routes, gates, gate_up, down_weight, old_map, new_map):
    experts, tensors = lax.axis_size("expert"), lax.axis_size("tensor")
    zs = experts // 4
    rows, part = tokens.shape
    _, width, _, hidden = gate_up.shape
    dma = pltpu.SemaphoreType.DMA
    mine = lax.axis_index("expert")
    lanes = -(-rows // 128) * 128
    table = jnp.pad(weights_of(routes, gates, old_map, new_map).T, ((0, 0), (0, lanes - rows)))
    every, tables = pl.pallas_call(
        functools.partial(gather_kernel, zs, rows),
        out_shape=(
            jax.ShapeDtypeStruct((experts * rows, tensors * part), tokens.dtype),
            jax.ShapeDtypeStruct((experts, experts, lanes), jnp.float32),
        ),
        in_specs=[pl.BlockSpec(memory_space=pl.ANY)] * 2,
        out_specs=[pl.BlockSpec(memory_space=pl.ANY)] * 2,
        scratch_shapes=[dma((2,)), dma((5, zs * 4, 3)), dma((2, zs * 4, 3))],
        compiler_params=pltpu.CompilerParams(
            collective_id=0, has_side_effects=True, vmem_limit_bytes=VMEM_BUDGET
        ),
        name="gather_tokens",
    )(tokens, table)
    share = lax.dynamic_index_in_dim(tables, mine, 1, keepdims=False)[:, :rows].reshape(-1, 1)
    projected = jnp.dot(
        every, gate_up.reshape(width, 2 * hidden), preferred_element_type=jnp.float32
    )
    gate, up = projected[:, :hidden], projected[:, hidden:]
    act = (jax.nn.silu(gate) * up).astype(jnp.bfloat16)
    w_out = down_weight.reshape(width, hidden)
    partial = share * lax.dot_general(
        act, w_out, (((1,), (1,)), ((), ())), preferred_element_type=jnp.float32
    )
    partial = partial.astype(jnp.bfloat16)
    half = rows // 2
    return pl.pallas_call(
        functools.partial(scatter_kernel, zs, rows),
        out_shape=jax.ShapeDtypeStruct((rows, part), jnp.bfloat16),
        in_specs=[pl.BlockSpec(memory_space=pl.ANY)],
        out_specs=pl.BlockSpec(memory_space=pltpu.VMEM),
        scratch_shapes=[
            pltpu.VMEM((zs * 4, 2, half, part), jnp.bfloat16),
            pltpu.VMEM((zs * 4, 2, half, part), jnp.bfloat16),
            pltpu.VMEM((zs * 2, 2, half, part), jnp.bfloat16),
            pltpu.VMEM((zs, 2, half, part), jnp.bfloat16),
            pltpu.VMEM((2, zs, 2, half, part), jnp.bfloat16),
            dma((4, zs * 4, 2)),
            dma((zs * 4, 2)),
            dma((zs * 4, 2)),
            dma((zs * 2, 2)),
            dma((zs, 2)),
            dma((2, zs, 2)),
        ],
        compiler_params=pltpu.CompilerParams(
            collective_id=1, has_side_effects=True, vmem_limit_bytes=VMEM_BUDGET
        ),
        name="scatter_sums",
    )(partial)


def routed(tokens, routes, gates, gate_up, down_weight, old_map, new_map):
    experts, tensors = lax.axis_size("expert"), lax.axis_size("tensor")
    rows, part = tokens.shape
    picks = routes.shape[1]
    capacity = (rows * picks + experts - 1) // experts
    _, width, _, hidden = gate_up.shape
    total = experts * capacity
    weight = weights_of(routes, gates, old_map, new_map)
    chosen = weights_of(routes, jnp.ones_like(gates), old_map, new_map)
    earlier = jnp.tril(jnp.ones((rows, rows), jnp.bfloat16), -1)
    position = jnp.dot(
        earlier, chosen.astype(jnp.bfloat16), preferred_element_type=jnp.float32
    ).astype(jnp.int32)
    hit = (position[:, :, None] == jnp.arange(capacity)) & (chosen[:, :, None] > 0)
    assign = hit.astype(jnp.bfloat16).reshape(rows, total)
    combine = jnp.where(hit, weight[:, :, None], 0.0).reshape(rows, total)
    outgoing = lax.dot_general(
        assign, tokens, (((0,), (0,)), ((), ())), preferred_element_type=jnp.float32
    )
    outgoing = outgoing.astype(jnp.bfloat16).reshape(experts, capacity, part)
    arrived = lax.all_to_all(outgoing, "expert", split_axis=0, concat_axis=0, tiled=True)
    piece = lax.all_gather(arrived, "tensor", axis=2, tiled=True).reshape(total, width)
    projected = jnp.dot(
        piece, gate_up.reshape(width, 2 * hidden), preferred_element_type=jnp.float32
    )
    act = (jax.nn.silu(projected[:, :hidden]) * projected[:, hidden:]).astype(jnp.bfloat16)
    down = lax.all_to_all(
        down_weight.reshape(tensors, part, hidden), "tensor", split_axis=0, concat_axis=2, tiled=True
    ).reshape(part, tensors * hidden)
    out = lax.dot_general(
        lax.all_gather(act, "tensor", axis=1, tiled=True),
        down,
        (((1,), (1,)), ((), ())),
        preferred_element_type=jnp.float32,
    )
    out = out.astype(jnp.bfloat16).reshape(experts, capacity, part)
    back = lax.all_to_all(out, "expert", split_axis=0, concat_axis=0, tiled=True)
    mixed = jnp.dot(
        combine,
        back.reshape(total, part).astype(jnp.float32),
        precision=lax.Precision.HIGHEST,
        preferred_element_type=jnp.float32,
    )
    return mixed.astype(jnp.bfloat16)


def local(*args):
    experts, tensors = lax.axis_size("expert"), lax.axis_size("tensor")
    rows, part = args[0].shape
    held = experts * rows * part * 2 * (tensors + 2)
    fits = tensors == 2 and experts % 4 == 0 and experts >= 8 and rows % 32 == 0
    if fits and held < VMEM_BUDGET:
        return gathered(*args)
    return routed(*args)


def solution(mesh):
    in_specs = (
        P(("dp", "expert"), "tensor"),
        P(("dp", "expert"), None),
        P(("dp", "expert"), None),
        P("expert", None, None, "tensor"),
        P("expert", None, "tensor"),
        P(),
        P(),
    )
    out_specs = P(("dp", "expert"), "tensor")
    return jax.shard_map(local, mesh=mesh, in_specs=in_specs, out_specs=out_specs, check_vma=False)
```
